32 devices in a mesh: groups: 2 (over x), ctx: 16 (over z, y, core).
Axes of the slice: x: 2, y: 2, z: 4, core: 2. Of those that a mesh axis runs over, the one named last changes fastest.
Arguments:
- sem_queries: bfloat16 [8192, 1024], P(('groups', 'ctx')), parts along dimension 0, may hold values from -170 to 170
- sem_keys: bfloat16 [8192, 1024], P(('groups', 'ctx')), parts along dimension 0, may hold values from -7 to 7
- sem_values: bfloat16 [8192, 1024], P(('groups', 'ctx')), parts along dimension 0, may hold values from -6 to 6
- sem_inputs: bfloat16 [8192, 2048], P(('groups', 'ctx')), parts along dimension 0, may hold values from -80 to 80
- out_proj: bfloat16 [1024, 2048], P('ctx'), may hold values from -0.5 to 0.5
- norm_gain: float32 [2048], replicated, may hold values from 0.1 to 1.9
- key_proj: bfloat16 [2048, 1024], P('ctx'), may hold values from -0.125 to 0.125
- value_proj: bfloat16 [2048, 1024], P('ctx'), may hold values from -0.125 to 0.125
- slopes: float32 [8], replicated, may hold values from 1 to 16
- coarse_queries: bfloat16 [32768, 1024], P(('groups', 'ctx')), parts along dimension 0, may hold values from -400 to 400
- counts: int32 [32], P(('groups', 'ctx')), parts along dimension 0, may hold values from 512 to 1024, as said below
- band_bounds: int32 [128, 2], P(('groups', 'ctx')), parts along dimension 0, may hold values from 0 to 4096, as said below
Outputs:
- coarse_context: bfloat16 [32768, 1024], P(('groups', 'ctx')), parts along dimension 0
The draws below stay inside these ranges and needn't reach their ends.
There are 2 independent parts, one for each index of `groups`. The reference program is written for one: setup_inputs(seed, part) draws one part's arguments, and reference() takes and returns one part's arrays. A program takes and returns all parts, laid end to end along the dimension named above; an argument that names none is the same for every part. Nothing has to cross between parts.
Inputs may be any that keep to these rules, and one draw needn't show every extreme that they name: `counts`: live coarse tokens of a ctx index fill its first slots; at least half of 1024; some index is full. `band_bounds`: a band of block n, held by ctx index c = n // 4, covers 512 // 2 to 512 rows and lies within the semantic rows of indices c - 1, c and c + 1; block 0 covers exactly 512.
All inputs are finite; a program needn't handle non-finite values.
Results may differ from the reference program's by a relative error of at most 0.0091.
Values may be sent and summed in bfloat16 or wider, within the bound.
A program may use at most 128 MiB of HBM per device.

```python
import math
import jax
import jax.numpy as jnp
from jax import lax

D = 2048
HEADS = 8
HEAD_DIM = 128
S_DEV = 256
W = 512
BAND = 512
CB = 256
HD = 1024
S_TOTAL = 4096
C_DEV = 1024
NB = 4
C_TOTAL = 16384


def paired_keys(key):
    key_base = jax.random.truncated_normal(jax.random.fold_in(key, 11), -6.0, 6.0, (S_TOTAL, HD), jnp.float32)
    query_base = jax.random.truncated_normal(jax.random.fold_in(key, 12), -6.0, 6.0, (S_TOTAL, HD), jnp.float32)
    return (query_base, key_base)


def draw_sem_queries(key, part):
    return paired_keys(key)[0].astype(jnp.bfloat16)


def draw_sem_keys(key, part):
    return paired_keys(key)[1].astype(jnp.bfloat16)


def draw_sem_inputs(key, part):
    base = jax.random.truncated_normal(jax.random.fold_in(key, 21), -4.0, 4.0, (S_TOTAL, D), jnp.float32)
    row_scale = jnp.exp(jax.random.uniform(jax.random.fold_in(key, 22), (S_TOTAL, 1), jnp.float32, -1.2, 1.1))
    column_scale = jnp.exp(jax.random.uniform(jax.random.fold_in(key, 23), (1, D), jnp.float32, -1.2, 1.1))
    return (base * row_scale * column_scale).astype(jnp.bfloat16)


def draw_coarse_queries(key, part):
    base = jax.random.truncated_normal(jax.random.fold_in(key, 41), -6.0, 6.0, (C_TOTAL, HD), jnp.float32)
    return base.astype(jnp.bfloat16)


def coarse_layout(key):
    device_total = S_TOTAL // S_DEV
    counts = jax.random.randint(jax.random.fold_in(key, 31), (device_total,), C_DEV // 2, C_DEV + 1)
    full_device = jax.random.randint(jax.random.fold_in(key, 32), (), 0, device_total)
    devices = jnp.arange(device_total)
    counts = jnp.where(devices == full_device, C_DEV, counts).astype(jnp.int32)
    starts = (jnp.cumsum(counts) - counts).astype(jnp.int32)
    blocks = jnp.arange(device_total * NB)
    owner_device = blocks // NB
    first_pos = starts[owner_device] + blocks % NB * CB
    center = (first_pos // 2 + CB // 4) * 2 // 3
    length = jax.random.randint(jax.random.fold_in(key, 33), (device_total * NB,), BAND // 2, BAND + 1)
    length = jnp.where(blocks == 0, BAND, length)
    jitter = jax.random.randint(jax.random.fold_in(key, 34), (device_total * NB,), -(BAND // 4), BAND // 4 + 1)
    lowest = jnp.maximum(owner_device - 1, 0) * S_DEV
    highest = jnp.minimum(owner_device + 2, device_total) * S_DEV
    band_low = jnp.clip(center - length // 2 + jitter, lowest, highest - length)
    return (counts, jnp.stack([band_low, band_low + length], axis=1).astype(jnp.int32))


def draw_counts(key, part):
    return coarse_layout(key)[0]


def draw_band_bounds(key, part):
    return coarse_layout(key)[1]


def shard_levels(key, dims, split, low, top_value):
    level, own = 1.0, jax.random.fold_in(key, 6)
    for position, shards_of in split:
        draws = jnp.exp(jax.random.uniform(jax.random.fold_in(own, position), (shards_of,), jnp.float32, low / len(split), top_value / len(split)))
        level = level * jnp.repeat(draws, dims[position] // shards_of).reshape([-1 if axis == position else 1 for axis in range(len(dims))])
    return level


def bell_draw(stream_key, dims, width, limit, cuts=(), kind=jnp.bfloat16):
    drawn = width * jax.random.normal(stream_key, dims, jnp.float32)
    if cuts:
        drawn = drawn * shard_levels(stream_key, dims, cuts, -0.22, 0.18)
    return jnp.clip(drawn, -limit, limit).astype(kind)


def setup_inputs(seed: int = 0, part: int = 0) -> dict:
    seeds = jax.random.split(jax.random.key(seed), 13)
    part_keys = jax.random.split(jax.random.fold_in(seeds[12], part), 13)
    sem_queries = draw_sem_queries(jax.random.fold_in(jax.random.fold_in(seeds[12], part), 71), part)
    sem_keys = draw_sem_keys(jax.random.fold_in(jax.random.fold_in(seeds[12], part), 71), part)
    sem_values = bell_draw(part_keys[2], (S_TOTAL, HD), 1.0, 6.0, ((0, 16),))
    sem_inputs = draw_sem_inputs(jax.random.fold_in(jax.random.fold_in(seeds[12], part), 71), part)
    out_proj = bell_draw(seeds[4], (HD, D), HEAD_DIM ** -0.5, 0.5, ((0, 16),))
    norm_gain = jnp.clip(1.0 + 0.18 * jax.random.normal(seeds[5], (D,), jnp.float32), 0.1, 1.9)
    key_proj = bell_draw(seeds[6], (D, HD), D ** -0.5, 0.125, ((0, 16),))
    value_proj = bell_draw(seeds[7], (D, HD), D ** -0.5, 0.125, ((0, 16),))
    slopes = jnp.clip(jnp.exp(jax.random.uniform(seeds[8], (HEADS,), jnp.float32, math.log(1.0), math.log(16.0))), 1.0, 16.0)
    coarse_queries = draw_coarse_queries(jax.random.fold_in(jax.random.fold_in(seeds[12], part), 71), part)
    counts = draw_counts(jax.random.fold_in(jax.random.fold_in(seeds[12], part), 71), part)
    band_bounds = draw_band_bounds(jax.random.fold_in(jax.random.fold_in(seeds[12], part), 71), part)
    return dict(sem_queries=sem_queries, sem_keys=sem_keys, sem_values=sem_values, sem_inputs=sem_inputs, out_proj=out_proj, norm_gain=norm_gain, key_proj=key_proj, value_proj=value_proj, slopes=slopes, coarse_queries=coarse_queries, counts=counts, band_bounds=band_bounds)


NEG_FILL = -1e+30

def head_split(matrix):
    return matrix.reshape(matrix.shape[0], HEADS, HEAD_DIM)

def attend(queries, key_rows, value_rows, allowed, time_bias):
    scores = jnp.einsum('qhd,khd->hqk', head_split(queries).astype(jnp.float32), head_split(key_rows).astype(jnp.float32)) * HEAD_DIM ** (-0.5)
    scores = jnp.where(allowed[None], scores + time_bias, NEG_FILL)
    largest = lax.optimization_barrier(jnp.max(scores, axis=2, keepdims=True))
    exponent = jnp.exp(scores - largest)
    weights = (exponent / lax.optimization_barrier(jnp.sum(exponent, axis=2, keepdims=True))).astype(jnp.bfloat16)
    blended = jnp.einsum('hqk,khd->qhd', weights.astype(jnp.float32), head_split(value_rows).astype(jnp.float32))
    return blended.reshape(queries.shape[0], -1)

def normalize(sem_stream, norm_gain):
    scaled = sem_stream * lax.rsqrt(lax.optimization_barrier(jnp.mean(sem_stream * sem_stream, axis=1, keepdims=True)) + 1e-05)
    return (scaled * norm_gain[None, :]).astype(jnp.bfloat16)

def cross_attend(queries, key_rows, value_rows, key_global, band_low, band_high, positions, slopes, live_rows):
    timing = (positions // 2).astype(jnp.float32) * (2.0 / 3.0)
    distance = jnp.abs(timing[:, None] - key_global[None, :].astype(jnp.float32))
    time_bias = -slopes[:, None, None] * distance[None] / BAND
    inside = (key_global >= band_low) & (key_global < band_high)
    allowed = jnp.broadcast_to(inside[None, :], (queries.shape[0], key_global.shape[0]))
    blended = attend(queries, key_rows, value_rows, allowed, time_bias)
    return jnp.where(live_rows[:, None], blended, 0.0).astype(jnp.bfloat16)

def reference(sem_queries, sem_keys, sem_values, sem_inputs, out_proj, norm_gain, key_proj, value_proj, slopes, coarse_queries, counts, band_bounds):
    padded_keys = jnp.concatenate([jnp.zeros((W, HD), jnp.bfloat16), sem_keys], axis=0)
    padded_values = jnp.concatenate([jnp.zeros((W, HD), jnp.bfloat16), sem_values], axis=0)

    def sem_block(block_index):
        first_row = block_index * S_DEV
        queries = lax.dynamic_slice_in_dim(sem_queries, first_row, S_DEV, 0)
        key_rows = lax.dynamic_slice_in_dim(padded_keys, first_row, S_DEV + W, 0)
        value_rows = lax.dynamic_slice_in_dim(padded_values, first_row, S_DEV + W, 0)
        query_global = first_row + jnp.arange(S_DEV, dtype=jnp.int32)
        key_global = first_row - W + jnp.arange(S_DEV + W, dtype=jnp.int32)
        key_lag = query_global[:, None] - key_global[None, :]
        allowed = (key_lag >= 0) & (key_lag < W) & (key_global[None, :] >= 0)
        return attend(queries, key_rows, value_rows, allowed, 0.0).astype(jnp.bfloat16)
    sem_att = lax.map(sem_block, jnp.arange(S_TOTAL // S_DEV, dtype=jnp.int32)).reshape(S_TOTAL, HD)
    sem_stream = sem_inputs.astype(jnp.float32) + jnp.dot(sem_att, out_proj, preferred_element_type=jnp.float32)
    normed = normalize(sem_stream, norm_gain)
    cross_keys = jnp.dot(normed, key_proj, preferred_element_type=jnp.float32).astype(jnp.bfloat16)
    cross_values = jnp.dot(normed, value_proj, preferred_element_type=jnp.float32).astype(jnp.bfloat16)
    stream_starts = (jnp.cumsum(counts) - counts).astype(jnp.int32)

    def coarse_block(block_index):
        owner_device = block_index // NB
        row_local = block_index % NB * CB + jnp.arange(CB, dtype=jnp.int32)
        band_low = band_bounds[block_index, 0]
        band_high = band_bounds[block_index, 1]
        first_key = jnp.minimum(band_low, S_TOTAL - BAND).astype(jnp.int32)
        key_rows = lax.dynamic_slice_in_dim(cross_keys, first_key, BAND, 0)
        value_rows = lax.dynamic_slice_in_dim(cross_values, first_key, BAND, 0)
        key_global = first_key + jnp.arange(BAND, dtype=jnp.int32)
        queries = lax.dynamic_slice_in_dim(coarse_queries, (block_index * CB).astype(jnp.int32), CB, 0)
        positions = stream_starts[owner_device] + row_local
        return cross_attend(queries, key_rows, value_rows, key_global, band_low, band_high, positions, slopes, row_local < counts[owner_device])
    return lax.map(coarse_block, jnp.arange(C_TOTAL // CB, dtype=jnp.int32)).reshape(C_TOTAL, HD)
```

```python
import jax
import jax.numpy as jnp
from jax import lax
from jax.experimental import pallas as pl
from jax.experimental.pallas import tpu as pltpu
from jax.sharding import PartitionSpec as P

HEADS = 8
HEAD_DIM = 128
W = 512
BAND = 512
CB = 256


NEG_FILL = -1e30


def passed_along(array, axis, by):
    length = lax.axis_size(axis)
    pairs = [(i, i + by) for i in range(length) if 0 <= i + by < length]
    return lax.ppermute(array, axis, pairs)


def carried_in(array, axis, combine, identity):
    length, position = (lax.axis_size(axis), lax.axis_index(axis))
    everything = lax.all_gather(array, axis)
    start = jnp.broadcast_to(jnp.asarray(identity, array.dtype), array.shape)

    def step(k, before):
        reached = k < position
        new = combine(before, everything[k])
        return jnp.where(reached, new, before)

    return lax.fori_loop(0, length, step, start)


def with_halo(array, sides, width):
    for axis, dim in sides:
        size, length = (lax.axis_size(axis), array.shape[dim])
        up = [(i, (i + 1) % size) for i in range(size - 1)]
        down = [(j, i) for i, j in up]
        last = lax.slice_in_dim(array, length - width, length, axis=dim)
        first = lax.slice_in_dim(array, 0, width, axis=dim)
        before = lax.ppermute(last, axis, up)
        after = lax.ppermute(first, axis, down)
        array = jnp.concatenate([before, array, after], axis=dim)
    return array


def head_split(matrix):
    return matrix.reshape(matrix.shape[0], HEADS, HEAD_DIM)


def attend(queries, key_rows, value_rows, allowed, time_bias):
    scores = jnp.einsum(
        "qhd,khd->hqk",
        head_split(queries),
        head_split(key_rows),
        preferred_element_type=jnp.float32,
    ) * HEAD_DIM ** (-0.5)
    scores = jnp.where(allowed[None], scores + time_bias, NEG_FILL)
    largest = jnp.max(scores, axis=2, keepdims=True)
    exponent = jnp.exp(scores - largest)
    weights = (exponent / jnp.sum(exponent, axis=2, keepdims=True)).astype(jnp.bfloat16)
    blended = jnp.einsum(
        "hqk,khd->qhd", weights, head_split(value_rows), preferred_element_type=jnp.float32
    )
    return blended.reshape(queries.shape[0], -1)


def normalize(sem_stream, norm_gain):
    scaled = sem_stream * lax.rsqrt(
        jnp.mean(sem_stream * sem_stream, axis=1, keepdims=True) + 1e-05
    )
    return (scaled * norm_gain[None, :]).astype(jnp.bfloat16)


LOG2E = 1.4426950408889634
SCALE2 = HEAD_DIM ** (-0.5) * LOG2E
SPAN = BAND + 16
MASKED = 1e30


def cross_kernel(bounds, meta, slopes, q_ref, k_ref, v_ref, o_ref, dist_ref):
    block = pl.program_id(0)
    stream_start, live, base = meta[0], meta[1], meta[2]
    low, high = bounds[block, 0], bounds[block, 1]
    near_rows = k_ref.shape[0]
    first = jnp.minimum((low - base) // 16 * 16, near_rows - SPAN)
    first = pl.multiple_of(first, 16)
    rows = pl.ds(first, SPAN)
    row_local = block * CB + lax.broadcasted_iota(jnp.int32, (1, CB), 1)
    timing = ((stream_start + row_local) // 2).astype(jnp.float32) * (2.0 / 3.0)
    key_global = base + first + lax.broadcasted_iota(jnp.int32, (SPAN, CB), 0)
    distance = jnp.abs(timing - key_global.astype(jnp.float32))
    inside = (key_global >= low) & (key_global < high)
    dist_ref[...] = jnp.where(inside, distance, MASKED)
    live_row = row_local < live
    for head in range(HEADS):
        cols = slice(head * HEAD_DIM, (head + 1) * HEAD_DIM)
        scores = lax.dot_general(
            k_ref[rows, cols], q_ref[:, cols], (((1,), (1,)), ((), ())),
            preferred_element_type=jnp.float32,
        )
        scores = scores * SCALE2 - dist_ref[...] * (slopes[head] * (LOG2E / BAND))
        exponent = jnp.exp2(scores - jnp.max(scores, axis=0, keepdims=True))
        total = jnp.sum(exponent, axis=0, keepdims=True)
        blended = lax.dot_general(
            v_ref[rows, cols], exponent.astype(jnp.bfloat16), (((0,), (0,)), ((), ())),
            preferred_element_type=jnp.float32,
        )
        blended = jnp.where(live_row, blended / total, 0.0)
        o_ref[:, cols] = blended.T.astype(jnp.bfloat16)


def cross_attention(bounds, meta, slopes, queries, near_keys, near_values):
    blocks, width = bounds.shape[0], queries.shape[1]
    whole = pl.BlockSpec(near_keys.shape, lambda b: (0, 0))
    smem = pl.BlockSpec(memory_space=pltpu.SMEM)
    return pl.pallas_call(
        cross_kernel,
        grid=(blocks,),
        in_specs=[smem, smem, smem, pl.BlockSpec((CB, width), lambda b: (b, 0)), whole, whole],
        out_specs=pl.BlockSpec((CB, width), lambda b: (b, 0)),
        out_shape=jax.ShapeDtypeStruct(queries.shape, jnp.bfloat16),
        scratch_shapes=[pltpu.VMEM((SPAN, CB), jnp.float32)],
        compiler_params=pltpu.CompilerParams(vmem_limit_bytes=48 * 1024 * 1024),
        cost_estimate=pl.CostEstimate(
            flops=4 * queries.shape[0] * SPAN * width, bytes_accessed=8 * 1024 * 1024,
            transcendentals=queries.shape[0] * SPAN * HEADS,
        ),
        name="cross_attention",
    )(bounds, meta, slopes, queries, near_keys, near_values)


def contract_rows(left_side, weight_piece):
    return jnp.dot(left_side, weight_piece, preferred_element_type=jnp.float32)


def add_counts(earlier_sum, later_sum):
    return earlier_sum + later_sum


def on_device(
    sem_queries,
    sem_keys,
    sem_values,
    sem_inputs,
    out_proj,
    norm_gain,
    key_proj,
    value_proj,
    slopes,
    coarse_queries,
    counts,
    band_bounds,
):
    rows_here = sem_queries.shape[0]
    device_index = lax.axis_index("ctx")
    own_pair = jnp.stack([sem_keys, sem_values])
    reach_shards = (W - 1 + rows_here - 1) // rows_here
    earlier = []
    for distance in range(1, reach_shards + 1):
        earlier.insert(0, passed_along(own_pair, "ctx", distance))
    window_pair = jnp.concatenate(earlier + [own_pair], axis=1)
    query_pos = jnp.arange(rows_here, dtype=jnp.int32)
    key_pos = jnp.arange(window_pair.shape[1], dtype=jnp.int32)
    key_lag = query_pos[:, None] + reach_shards * rows_here - key_pos[None, :]
    key_global = device_index * rows_here - reach_shards * rows_here + key_pos
    allowed = (key_lag >= 0) & (key_lag < W) & (key_global[None, :] >= 0)
    sem_att = attend(sem_queries, window_pair[0], window_pair[1], allowed, 0.0).astype(jnp.bfloat16)
    projected = contract_rows(sem_att, lax.all_gather(out_proj, "ctx", axis=0, tiled=True))
    sem_stream = sem_inputs.astype(jnp.float32) + projected
    normed = normalize(sem_stream, norm_gain)
    key_sum = contract_rows(normed, lax.all_gather(key_proj, "ctx", axis=0, tiled=True))
    value_sum = contract_rows(normed, lax.all_gather(value_proj, "ctx", axis=0, tiled=True))
    cross_keys = key_sum.astype(jnp.bfloat16)
    cross_values = value_sum.astype(jnp.bfloat16)
    stream_start = carried_in(counts, "ctx", add_counts, jnp.zeros_like(counts))[0]
    near_pair = with_halo(jnp.stack([cross_keys, cross_values]), (("ctx", 1),), rows_here)
    base_row = (device_index - 1) * rows_here
    meta = jnp.stack([stream_start, counts[0], base_row]).astype(jnp.int32)
    return cross_attention(band_bounds, meta, slopes, coarse_queries, near_pair[0], near_pair[1])


def solution(mesh):
    return jax.shard_map(
        on_device,
        mesh=mesh,
        in_specs=(
            P(("groups", "ctx"), None),
            P(("groups", "ctx"), None),
            P(("groups", "ctx"), None),
            P(("groups", "ctx"), None),
            P("ctx", None),
            P(),
            P("ctx", None),
            P("ctx", None),
            P(),
            P(("groups", "ctx"), None),
            P(("groups", "ctx")),
            P(("groups", "ctx"), None),
        ),
        out_specs=P(("groups", "ctx"), None),
        check_vma=False,
    )
```

```python
import functools

import jax
import jax.numpy as jnp
from jax import lax
from jax.experimental import pallas as pl
from jax.experimental.pallas import tpu as pltpu
from jax.sharding import PartitionSpec as P

HEADS = 8
HEAD_DIM = 128
W = 512
BAND = 512
CB = 256


LOG2E = 1.4426950408889634
SCALE2 = HEAD_DIM ** (-0.5) * LOG2E
SPAN = BAND + 16
MASKED = 1e30


def cross_kernel(bounds, start, counts, slopes, q_ref, k_ref, v_ref, o_ref, dist_ref):
    block = pl.program_id(0)
    stream_start, live = start[0, 0], counts[0]
    low, high = bounds[block, 0], bounds[block, 1]
    near_rows = k_ref.shape[0]
    base = (lax.axis_index("ctx") - 1) * (near_rows // 3)
    first = jnp.minimum((low - base) // 16 * 16, near_rows - SPAN)
    first = pl.multiple_of(first, 16)
    rows = pl.ds(first, SPAN)
    row_local = block * CB + lax.broadcasted_iota(jnp.int32, (1, CB), 1)
    timing = ((stream_start + row_local) // 2).astype(jnp.float32) * (2.0 / 3.0)
    key_global = base + first + lax.broadcasted_iota(jnp.int32, (SPAN, CB), 0)
    distance = jnp.abs(timing - key_global.astype(jnp.float32))
    inside = (key_global >= low) & (key_global < high)
    dist_ref[...] = jnp.where(inside, distance, MASKED)
    live_row = row_local < live
    for head in range(HEADS):
        cols = slice(head * HEAD_DIM, (head + 1) * HEAD_DIM)
        scores = lax.dot_general(
            k_ref[rows, cols], q_ref[:, cols], (((1,), (1,)), ((), ())),
            preferred_element_type=jnp.float32,
        )
        scores = scores * SCALE2 - dist_ref[...] * (slopes[head] * (LOG2E / BAND))
        exponent = jnp.exp2(scores - jnp.max(scores, axis=0, keepdims=True))
        total = jnp.sum(exponent, axis=0, keepdims=True)
        blended = lax.dot_general(
            v_ref[rows, cols], exponent.astype(jnp.bfloat16), (((0,), (0,)), ((), ())),
            preferred_element_type=jnp.float32,
        )
        blended = jnp.where(live_row, blended / total, 0.0)
        o_ref[:, cols] = blended.T.astype(jnp.bfloat16)


def cross_attention(bounds, start, counts, slopes, queries, near_keys, near_values):
    blocks, width = bounds.shape[0], queries.shape[1]
    whole = pl.BlockSpec(near_keys.shape, lambda b: (0, 0))
    smem = pl.BlockSpec(memory_space=pltpu.SMEM)
    return pl.pallas_call(
        cross_kernel,
        grid=(blocks,),
        in_specs=[smem, smem, smem, smem, pl.BlockSpec((CB, width), lambda b: (b, 0)), whole, whole],
        out_specs=pl.BlockSpec((CB, width), lambda b: (b, 0)),
        out_shape=jax.ShapeDtypeStruct(queries.shape, jnp.bfloat16),
        scratch_shapes=[pltpu.VMEM((SPAN, CB), jnp.float32)],
        compiler_params=pltpu.CompilerParams(vmem_limit_bytes=48 * 1024 * 1024),
        cost_estimate=pl.CostEstimate(
            flops=4 * queries.shape[0] * SPAN * width, bytes_accessed=8 * 1024 * 1024,
            transcendentals=queries.shape[0] * SPAN * HEADS,
        ),
        name="cross_attention",
    )(bounds, start, counts, slopes, queries, near_keys, near_values)


def ring_position(index, n):
    chips, chip, core = n // 2, index // 2, index % 2
    odd = chip % 2
    return ((1 - odd) * (chip // 2) + odd * (chips - 1 - chip // 2)) * 2 + core


def ring_index(position, n):
    position = (position + n) % n
    chips, place, core = n // 2, position // 2, position % 2
    back = place // (chips // 2)
    return ((1 - back) * 2 * place + back * (2 * (chips - 1 - place) + 1)) * 2 + core


def semantic_kernel(
    n, q_ref, k_ref, v_ref, x_ref, gain_ref, wo_ref, wk_ref, wv_ref, count_ref,
    near_k, near_v, start_ref,
    win_k, win_v, all_o, all_k, all_v, all_c, att, stream, normed, mask,
    ring_send, ring_recv, sem_send, sem_recv, near_send, near_recv,
):
    me = lax.axis_index("ctx")
    rows = q_ref.shape[0]
    reach = win_k.shape[0] // rows - 1
    spot = ring_position(me, n)
    after, before = ring_index(spot + 1, n), ring_index(spot + n - 1, n)
    steps = (n // 2, n - 1 - n // 2)

    barrier = pltpu.get_barrier_semaphore()
    partners = [after, before]
    for far in range(1, reach + 1):
        partners += [(me + far) % n, (me + n - far) % n]
    for partner in partners:
        pl.semaphore_signal(
            barrier, inc=1, device_id={"ctx": partner}, device_id_type=pl.DeviceIdType.MESH
        )
    pl.semaphore_wait(barrier, len(partners))

    def send(src, dst, sems, place, target):
        return pltpu.make_async_remote_copy(
            src_ref=src, dst_ref=dst, send_sem=sems[0].at[place], recv_sem=sems[1].at[place],
            device_id={"ctx": target}, device_id_type=pl.DeviceIdType.MESH,
        )

    half_o = all_o.shape[1] // 2
    pieces = [
        (all_o, slice(0, half_o)), (all_o, slice(half_o, 2 * half_o)), (all_c, slice(0, 128)),
        (all_k, slice(0, all_k.shape[1])), (all_v, slice(0, all_v.shape[1])),
    ]

    def ring(piece, way, step, arriving=False):
        ref, cols = pieces[piece]
        depth = ref.shape[0] // n
        back = step + 1 if arriving else step
        owner = ring_index(spot + n - back if way == 0 else spot + back, n)
        part = ref.at[pl.ds(pl.multiple_of(owner * depth, depth), depth), cols]
        place = (piece * 2 + way) * steps[0] + step
        return send(part, part, (ring_send, ring_recv), place, after if way == 0 else before)

    def begin(group):
        for piece in group:
            for way in (0, 1):
                ring(piece, way, 0).start()

    def forward(group, step):
        for piece in group:
            for way in (0, 1):
                ring(piece, way, step, True).wait_recv()
                ring(piece, way, step + 1).start()

    def finish(group):
        last = steps[0] - 1
        for piece in group:
            ring(piece, 0, last - 1, True).wait_recv()
            ring(piece, 0, last).start()
            ring(piece, 1, last - 1, True).wait_recv()
        for piece in group:
            ring(piece, 0, last, True).wait_recv()

    first_group, second_group = (0, 1, 2), (3, 4)
    for full, own in ((all_o, wo_ref), (all_k, wk_ref), (all_v, wv_ref), (all_c, count_ref)):
        depth = own.shape[0]
        full[pl.ds(pl.multiple_of(me * depth, depth), depth), :] = own[...]
    here = pl.ds(reach * rows, rows)
    win_k[here, :] = k_ref[...]
    win_v[here, :] = v_ref[...]

    def window_copies(far):
        there = pl.ds((reach - far) * rows, rows)
        target = (me + far) % n
        return [
            send(win.at[here], win.at[there], (sem_send, sem_recv), 2 * (far - 1) + i, target)
            for i, win in enumerate((win_k, win_v))
        ]

    def window_start(far):
        @pl.when(me + far < n)
        def _():
            for copy in window_copies(far):
                copy.start()

        @pl.when(me < far)
        def _():
            there = pl.ds((reach - far) * rows, rows)
            win_k[there, :] = jnp.zeros((rows, win_k.shape[1]), jnp.bfloat16)
            win_v[there, :] = jnp.zeros((rows, win_v.shape[1]), jnp.bfloat16)

    begin(first_group)
    for far in range(1, reach + 1):
        window_start(far)

    key_row = lax.broadcasted_iota(jnp.int32, mask.shape, 0)
    lag = lax.broadcasted_iota(jnp.int32, mask.shape, 1) + reach * rows - key_row
    allowed = (lag >= 0) & (lag < W) & (key_row + (me - reach) * rows >= 0)
    mask[...] = jnp.where(allowed, 0.0, -MASKED)

    def first_step(step, carry):
        forward(first_group, step)
        return carry

    lax.fori_loop(0, steps[0] - 2, first_step, 0)
    begin(second_group)
    finish(first_group)

    for far in range(1, reach + 1):
        @pl.when(me >= far)
        def _():
            for copy in window_copies(far):
                copy.wait_recv()

    def attend_head(head):
        cols = pl.ds(pl.multiple_of(head * HEAD_DIM, HEAD_DIM), HEAD_DIM)
        scores = lax.dot_general(
            win_k[:, cols], q_ref[:, cols], (((1,), (1,)), ((), ())),
            preferred_element_type=jnp.float32,
        )
        scores = scores * SCALE2 + mask[...]
        exponent = jnp.exp2(scores - jnp.max(scores, axis=0, keepdims=True))
        total = jnp.sum(exponent, axis=0, keepdims=True)
        blended = lax.dot_general(
            win_v[:, cols], exponent.astype(jnp.bfloat16), (((0,), (0,)), ((), ())),
            preferred_element_type=jnp.float32,
        )
        att[:, cols] = (blended / total).T.astype(jnp.bfloat16)

    per_step = HEADS // 4

    def second_step(step, carry):
        forward(second_group, step)
        for k in range(per_step):
            attend_head(step * per_step + k)
        return carry

    lax.fori_loop(0, 4, second_step, 0)

    width = stream.shape[1]
    squares = jnp.zeros((rows, 1), jnp.float32)
    for col in range(0, width, 512):
        cols = slice(col, col + 512)
        value = x_ref[:, cols].astype(jnp.float32) + jnp.dot(
            att[...], all_o[:, cols], preferred_element_type=jnp.float32
        )
        stream[:, cols] = value
        squares = squares + jnp.sum(value * value, axis=1, keepdims=True)
    inverse = lax.rsqrt(squares / width + 1e-05)
    normed[...] = (stream[...] * inverse * gain_ref[...]).astype(jnp.bfloat16)

    def last_step(step, carry):
        forward(second_group, step)
        return carry

    lax.fori_loop(4, steps[0] - 2, last_step, 0)
    finish(second_group)

    def near_copies(i, near, way):
        there = pl.ds((1 - way) * 2 * rows, rows)
        there = pl.ds(0, rows) if way == 0 else pl.ds(2 * rows, rows)
        target = (me + 1) % n if way == 0 else (me + n - 1) % n
        return send(
            near.at[pl.ds(rows, rows)], near.at[there], (near_send, near_recv), 2 * i + way, target
        )

    for i, (near, weight) in enumerate(((near_k, all_k), (near_v, all_v))):
        for col in range(0, near.shape[1], 512):
            cols = slice(col, col + 512)
            near[pl.ds(rows, rows), cols] = jnp.dot(
                normed[...], weight[:, cols], preferred_element_type=jnp.float32
            ).astype(jnp.bfloat16)

        @pl.when(me < n - 1)
        def _():
            near_copies(i, near, 0).start()

        @pl.when(me >= 1)
        def _():
            near_copies(i, near, 1).start()

        @pl.when(me == 0)
        def _():
            near[pl.ds(0, rows), :] = jnp.zeros((rows, near.shape[1]), jnp.bfloat16)

        @pl.when(me == n - 1)
        def _():
            near[pl.ds(2 * rows, rows), :] = jnp.zeros((rows, near.shape[1]), jnp.bfloat16)

    counted = lax.broadcasted_iota(jnp.int32, all_c.shape, 0)
    taken = (counted % 8 == 0) & (counted // 8 < me)
    earlier = jnp.sum(jnp.where(taken, all_c[...], 0), axis=0, keepdims=True)
    start_ref[...] = jnp.broadcast_to(earlier, start_ref.shape)

    def sent(step, carry):
        for piece in range(len(pieces)):
            for way in (0, 1):
                ring(piece, way, step).wait_send()
        return carry

    lax.fori_loop(0, steps[1], sent, 0)
    for piece in range(len(pieces)):
        ring(piece, 0, steps[0] - 1).wait_send()
    for far in range(1, reach + 1):
        @pl.when(me + far < n)
        def _():
            for copy in window_copies(far):
                copy.wait_send()
    for i, near in enumerate((near_k, near_v)):
        @pl.when(me < n - 1)
        def _():
            near_copies(i, near, 0).wait_send()
            near_copies(i, near, 1).wait_recv()

        @pl.when(me >= 1)
        def _():
            near_copies(i, near, 1).wait_send()
            near_copies(i, near, 0).wait_recv()


def semantic_part(n, queries, keys, values, inputs, gain, out_proj, key_proj, value_proj, counts):
    rows, width = queries.shape
    model = inputs.shape[1]
    reach = (W - 1 + rows - 1) // rows
    bf16, f32 = jnp.bfloat16, jnp.float32
    window = (reach + 1) * rows
    ring_sems = 5 * 2 * (n // 2)
    vmem = pl.BlockSpec(memory_space=pltpu.VMEM)
    dma = pltpu.SemaphoreType.DMA
    return pl.pallas_call(
        functools.partial(semantic_kernel, n),
        in_specs=[vmem] * 9,
        out_specs=[vmem] * 3,
        out_shape=[
            jax.ShapeDtypeStruct((3 * rows, width), bf16),
            jax.ShapeDtypeStruct((3 * rows, width), bf16),
            jax.ShapeDtypeStruct((8, 128), jnp.int32),
        ],
        scratch_shapes=[
            pltpu.VMEM((window, width), bf16),
            pltpu.VMEM((window, width), bf16),
            pltpu.VMEM((n * out_proj.shape[0], model), bf16),
            pltpu.VMEM((n * key_proj.shape[0], width), bf16),
            pltpu.VMEM((n * value_proj.shape[0], width), bf16),
            pltpu.VMEM((n * 8, 128), jnp.int32),
            pltpu.VMEM((rows, width), bf16),
            pltpu.VMEM((rows, model), f32),
            pltpu.VMEM((rows, model), bf16),
            pltpu.VMEM((window, rows), f32),
            dma((ring_sems,)), dma((ring_sems,)),
            dma((2 * reach,)), dma((2 * reach,)),
            dma((4,)), dma((4,)),
        ],
        compiler_params=pltpu.CompilerParams(
            collective_id=0, has_side_effects=True, vmem_limit_bytes=48 * 1024 * 1024
        ),
        cost_estimate=pl.CostEstimate(
            flops=2 * rows * width * (2 * window + 3 * model), bytes_accessed=8 * 1024 * 1024,
            transcendentals=rows * window * HEADS,
        ),
        name="semantic_part",
    )(queries, keys, values, inputs, gain, out_proj, key_proj, value_proj, counts)


def on_device(
    n, sem_queries, sem_keys, sem_values, sem_inputs, out_proj, norm_gain, key_proj, value_proj,
    slopes, coarse_queries, counts, band_bounds,
):
    near_keys, near_values, start = semantic_part(
        n, sem_queries, sem_keys, sem_values, sem_inputs, norm_gain[None, :], out_proj, key_proj,
        value_proj, jnp.broadcast_to(counts[:, None], (8, 128)),
    )
    return cross_attention(
        band_bounds, start, counts, slopes, coarse_queries, near_keys, near_values
    )


def solution(mesh):
    return jax.shard_map(
        functools.partial(on_device, mesh.shape["ctx"]),
        mesh=mesh,
        in_specs=(
            P(("groups", "ctx"), None),
            P(("groups", "ctx"), None),
            P(("groups", "ctx"), None),
            P(("groups", "ctx"), None),
            P("ctx", None),
            P(),
            P("ctx", None),
            P("ctx", None),
            P(),
            P(("groups", "ctx"), None),
            P(("groups", "ctx")),
            P(("groups", "ctx"), None),
        ),
        out_specs=P(("groups", "ctx"), None),
        check_vma=False,
    )
```

```python
import functools

import jax
import jax.numpy as jnp
from jax import lax
from jax.experimental import pallas as pl
from jax.experimental.pallas import tpu as pltpu
from jax.sharding import PartitionSpec as P

HEADS = 8
HEAD_DIM = 128
W = 512
BAND = 512
CB = 256


LOG2E = 1.4426950408889634
SCALE2 = HEAD_DIM ** (-0.5) * LOG2E
SPAN = BAND + 16
MASKED = 1e30


def cross_kernel(bounds, start, counts, slopes, q_ref, k_ref, v_ref, o_ref, dist_ref):
    block = pl.program_id(0)
    stream_start, live = start[0, 0], counts[0]
    low, high = bounds[block, 0], bounds[block, 1]
    near_rows = k_ref.shape[0]
    base = (lax.axis_index("ctx") - 1) * (near_rows // 3)
    first = jnp.minimum((low - base) // 16 * 16, near_rows - SPAN)
    first = pl.multiple_of(first, 16)
    rows = pl.ds(first, SPAN)
    row_local = block * CB + lax.broadcasted_iota(jnp.int32, (1, CB), 1)
    timing = ((stream_start + row_local) // 2).astype(jnp.float32) * (2.0 / 3.0)
    key_global = base + first + lax.broadcasted_iota(jnp.int32, (SPAN, CB), 0)
    distance = jnp.abs(timing - key_global.astype(jnp.float32))
    inside = (key_global >= low) & (key_global < high)
    dist_ref[...] = jnp.where(inside, distance, MASKED)
    live_row = row_local < live
    for head in range(HEADS):
        cols = slice(head * HEAD_DIM, (head + 1) * HEAD_DIM)
        scores = lax.dot_general(
            k_ref[rows, cols], q_ref[:, cols], (((1,), (1,)), ((), ())),
            preferred_element_type=jnp.float32,
        )
        scores = scores * SCALE2 - dist_ref[...] * (slopes[head] * (LOG2E / BAND))
        exponent = jnp.exp2(scores - jnp.max(scores, axis=0, keepdims=True))
        total = jnp.sum(exponent, axis=0, keepdims=True)
        blended = lax.dot_general(
            v_ref[rows, cols], exponent.astype(jnp.bfloat16), (((0,), (0,)), ((), ())),
            preferred_element_type=jnp.float32,
        )
        blended = jnp.where(live_row, blended / total, 0.0)
        o_ref[:, cols] = blended.T.astype(jnp.bfloat16)


def cross_attention(bounds, start, counts, slopes, queries, near_keys, near_values):
    blocks, width = bounds.shape[0], queries.shape[1]
    whole = pl.BlockSpec(near_keys.shape, lambda b: (0, 0))
    smem = pl.BlockSpec(memory_space=pltpu.SMEM)
    return pl.pallas_call(
        cross_kernel,
        grid=(blocks,),
        in_specs=[smem, smem, smem, smem, pl.BlockSpec((CB, width), lambda b: (b, 0)), whole, whole],
        out_specs=pl.BlockSpec((CB, width), lambda b: (b, 0)),
        out_shape=jax.ShapeDtypeStruct(queries.shape, jnp.bfloat16),
        scratch_shapes=[pltpu.VMEM((SPAN, CB), jnp.float32)],
        compiler_params=pltpu.CompilerParams(vmem_limit_bytes=48 * 1024 * 1024),
        cost_estimate=pl.CostEstimate(
            flops=4 * queries.shape[0] * SPAN * width, bytes_accessed=8 * 1024 * 1024,
            transcendentals=queries.shape[0] * SPAN * HEADS,
        ),
        name="cross_attention",
    )(bounds, start, counts, slopes, queries, near_keys, near_values)


def ring_position(index, n):
    chips, chip, core = n // 2, index // 2, index % 2
    odd = chip % 2
    return ((1 - odd) * (chip // 2) + odd * (chips - 1 - chip // 2)) * 2 + core


def ring_index(position, n):
    position = (position + n) % n
    chips, place, core = n // 2, position // 2, position % 2
    back = place // (chips // 2)
    return ((1 - back) * 2 * place + back * (2 * (chips - 1 - place) + 1)) * 2 + core


def semantic_kernel(
    n, q_hbm, k_hbm, v_hbm, x_hbm, gain_ref, wo_ref, wk_ref, wv_ref, count_ref,
    near_k, near_v, start_ref,
    q_ref, x_ref, load_sem, win_k, win_v, all_o, all_k, all_v, all_c, att, stream, normed, mask,
    ring_send, ring_recv, sem_send, sem_recv, near_send, near_recv,
):
    me = lax.axis_index("ctx")
    rows = q_ref.shape[0]
    reach = win_k.shape[0] // rows - 1
    spot = ring_position(me, n)
    after, before = ring_index(spot + 1, n), ring_index(spot + n - 1, n)
    steps = (n // 2, n - 1 - n // 2)

    here = pl.ds(reach * rows, rows)
    loads = [(k_hbm, win_k.at[here]), (v_hbm, win_v.at[here])]
    for own, full in ((wo_ref, all_o), (wk_ref, all_k), (wv_ref, all_v)):
        depth = own.shape[0]
        loads.append((own, full.at[pl.ds(pl.multiple_of(me * depth, depth), depth)]))
    loads += [(q_hbm, q_ref), (x_hbm, x_ref)]
    loads = [pltpu.make_async_copy(a, b, load_sem.at[i]) for i, (a, b) in enumerate(loads)]
    for load in loads:
        load.start()

    barrier = pltpu.get_barrier_semaphore()
    partners = [after, before]
    for far in range(1, reach + 1):
        partners += [(me + far) % n, (me + n - far) % n]
    for partner in partners:
        pl.semaphore_signal(
            barrier, inc=1, device_id={"ctx": partner}, device_id_type=pl.DeviceIdType.MESH
        )
    pl.semaphore_wait(barrier, len(partners))

    def send(src, dst, sems, place, target):
        return pltpu.make_async_remote_copy(
            src_ref=src, dst_ref=dst, send_sem=sems[0].at[place], recv_sem=sems[1].at[place],
            device_id={"ctx": target}, device_id_type=pl.DeviceIdType.MESH,
        )

    half_o = all_o.shape[1] // 2
    pieces = [
        (all_o, slice(0, half_o)), (all_o, slice(half_o, 2 * half_o)), (all_c, slice(0, 128)),
        (all_k, slice(0, all_k.shape[1])), (all_v, slice(0, all_v.shape[1])),
    ]

    def ring(piece, way, step, arriving=False):
        ref, cols = pieces[piece]
        depth = ref.shape[0] // n
        back = step + 1 if arriving else step
        owner = ring_index(spot + n - back if way == 0 else spot + back, n)
        part = ref.at[pl.ds(pl.multiple_of(owner * depth, depth), depth), cols]
        place = (piece * 2 + way) * steps[0] + step
        return send(part, part, (ring_send, ring_recv), place, after if way == 0 else before)

    def begin(group):
        for piece in group:
            for way in (0, 1):
                ring(piece, way, 0).start()

    def forward(group, step):
        for piece in group:
            for way in (0, 1):
                ring(piece, way, step, True).wait_recv()
                ring(piece, way, step + 1).start()

    def finish(group):
        last = steps[0] - 1
        for piece in group:
            ring(piece, 0, last - 1, True).wait_recv()
            ring(piece, 0, last).start()
            ring(piece, 1, last - 1, True).wait_recv()
        for piece in group:
            ring(piece, 0, last, True).wait_recv()

    first_group, second_group = (0, 1, 2), (3, 4)
    all_c[pl.ds(pl.multiple_of(me * 8, 8), 8), :] = count_ref[...]

    slots = [pl.ds((reach - far) * rows, rows) for far in range(reach + 1)]

    def window_copies(route):
        target = (me + (2 if route == 1 else 1)) % n
        return [
            send(
                win.at[slots[1 if route == 2 else 0]], win.at[slots[2 if route else 1]],
                (sem_send, sem_recv), 2 * route + i, target,
            )
            for i, win in enumerate((win_k, win_v))
        ]

    even = me % 2 == 0
    sends = (me < n - 1, even & (me < n - 2), even & (me >= 2))
    receives = (me >= 1, even & (me >= 2), (me % 2 == 1) & (me >= 3))

    def window_do(route, when, action):
        @pl.when(when[route])
        def _():
            for copy in window_copies(route):
                getattr(copy, action)()

    for far in range(1, reach + 1):
        @pl.when(me < far)
        def _():
            win_k[slots[far], :] = jnp.zeros((rows, win_k.shape[1]), jnp.bfloat16)
            win_v[slots[far], :] = jnp.zeros((rows, win_v.shape[1]), jnp.bfloat16)

    for load in loads[2:3] + loads[:2]:
        load.wait()
    begin(first_group)
    window_do(0, sends, "start")
    window_do(1, sends, "start")
    for load in loads[3:]:
        load.wait()

    key_row = lax.broadcasted_iota(jnp.int32, mask.shape, 0)
    lag = lax.broadcasted_iota(jnp.int32, mask.shape, 1) + reach * rows - key_row
    allowed = (lag >= 0) & (lag < W) & (key_row + (me - reach) * rows >= 0)
    mask[...] = jnp.where(allowed, 0.0, -MASKED)

    def first_step(step, carry):
        forward(first_group, step)
        return carry

    lax.fori_loop(0, steps[0] - 2, first_step, 0)
    window_do(0, receives, "wait_recv")
    window_do(2, sends, "start")
    begin(second_group)
    finish(first_group)

    window_do(1, receives, "wait_recv")
    window_do(2, receives, "wait_recv")

    def attend_head(head):
        cols = pl.ds(pl.multiple_of(head * HEAD_DIM, HEAD_DIM), HEAD_DIM)
        scores = lax.dot_general(
            win_k[:, cols], q_ref[:, cols], (((1,), (1,)), ((), ())),
            preferred_element_type=jnp.float32,
        )
        scores = scores * SCALE2 + mask[...]
        exponent = jnp.exp2(scores - jnp.max(scores, axis=0, keepdims=True))
        total = jnp.sum(exponent, axis=0, keepdims=True)
        blended = lax.dot_general(
            win_v[:, cols], exponent.astype(jnp.bfloat16), (((0,), (0,)), ((), ())),
            preferred_element_type=jnp.float32,
        )
        att[:, cols] = (blended / total).T.astype(jnp.bfloat16)

    per_step = HEADS // 4

    def second_step(step, carry):
        forward(second_group, step)
        for k in range(per_step):
            attend_head(step * per_step + k)
        return carry

    lax.fori_loop(0, 4, second_step, 0)

    width = stream.shape[1]
    squares = jnp.zeros((rows, 1), jnp.float32)
    for col in range(0, width, 512):
        cols = slice(col, col + 512)
        value = x_ref[:, cols].astype(jnp.float32) + jnp.dot(
            att[...], all_o[:, cols], preferred_element_type=jnp.float32
        )
        stream[:, cols] = value
        squares = squares + jnp.sum(value * value, axis=1, keepdims=True)
    inverse = lax.rsqrt(squares / width + 1e-05)
    normed[...] = (stream[...] * inverse * gain_ref[...]).astype(jnp.bfloat16)

    def last_step(step, carry):
        forward(second_group, step)
        return carry

    lax.fori_loop(4, steps[0] - 2, last_step, 0)
    finish(second_group)

    def near_copies(i, near, way):
        there = pl.ds((1 - way) * 2 * rows, rows)
        there = pl.ds(0, rows) if way == 0 else pl.ds(2 * rows, rows)
        target = (me + 1) % n if way == 0 else (me + n - 1) % n
        return send(
            near.at[pl.ds(rows, rows)], near.at[there], (near_send, near_recv), 2 * i + way, target
        )

    for i, (near, weight) in enumerate(((near_k, all_k), (near_v, all_v))):
        for col in range(0, near.shape[1], 512):
            cols = slice(col, col + 512)
            near[pl.ds(rows, rows), cols] = jnp.dot(
                normed[...], weight[:, cols], preferred_element_type=jnp.float32
            ).astype(jnp.bfloat16)

        @pl.when(me < n - 1)
        def _():
            near_copies(i, near, 0).start()

        @pl.when(me >= 1)
        def _():
            near_copies(i, near, 1).start()

        @pl.when(me == 0)
        def _():
            near[pl.ds(0, rows), :] = jnp.zeros((rows, near.shape[1]), jnp.bfloat16)

        @pl.when(me == n - 1)
        def _():
            near[pl.ds(2 * rows, rows), :] = jnp.zeros((rows, near.shape[1]), jnp.bfloat16)

    counted = lax.broadcasted_iota(jnp.int32, all_c.shape, 0)
    taken = (counted % 8 == 0) & (counted // 8 < me)
    earlier = jnp.sum(jnp.where(taken, all_c[...], 0), axis=0, keepdims=True)
    start_ref[...] = jnp.broadcast_to(earlier, start_ref.shape)

    def sent(step, carry):
        for piece in range(len(pieces)):
            for way in (0, 1):
                ring(piece, way, step).wait_send()
        return carry

    lax.fori_loop(0, steps[1], sent, 0)
    for piece in range(len(pieces)):
        ring(piece, 0, steps[0] - 1).wait_send()
    for route in range(3):
        window_do(route, sends, "wait_send")
    for i, near in enumerate((near_k, near_v)):
        @pl.when(me < n - 1)
        def _():
            near_copies(i, near, 0).wait_send()
            near_copies(i, near, 1).wait_recv()

        @pl.when(me >= 1)
        def _():
            near_copies(i, near, 1).wait_send()
            near_copies(i, near, 0).wait_recv()


def semantic_part(n, queries, keys, values, inputs, gain, out_proj, key_proj, value_proj, counts):
    rows, width = queries.shape
    model = inputs.shape[1]
    reach = (W - 1 + rows - 1) // rows
    bf16, f32 = jnp.bfloat16, jnp.float32
    window = (reach + 1) * rows
    ring_sems = 5 * 2 * (n // 2)
    vmem = pl.BlockSpec(memory_space=pltpu.VMEM)
    hbm = pl.BlockSpec(memory_space=pl.ANY)
    dma = pltpu.SemaphoreType.DMA
    return pl.pallas_call(
        functools.partial(semantic_kernel, n),
        in_specs=[hbm] * 4 + [vmem] + [hbm] * 3 + [vmem],
        out_specs=[vmem] * 3,
        out_shape=[
            jax.ShapeDtypeStruct((3 * rows, width), bf16),
            jax.ShapeDtypeStruct((3 * rows, width), bf16),
            jax.ShapeDtypeStruct((8, 128), jnp.int32),
        ],
        scratch_shapes=[
            pltpu.VMEM((rows, width), bf16),
            pltpu.VMEM((rows, model), bf16),
            dma((7,)),
            pltpu.VMEM((window, width), bf16),
            pltpu.VMEM((window, width), bf16),
            pltpu.VMEM((n * out_proj.shape[0], model), bf16),
            pltpu.VMEM((n * key_proj.shape[0], width), bf16),
            pltpu.VMEM((n * value_proj.shape[0], width), bf16),
            pltpu.VMEM((n * 8, 128), jnp.int32),
            pltpu.VMEM((rows, width), bf16),
            pltpu.VMEM((rows, model), f32),
            pltpu.VMEM((rows, model), bf16),
            pltpu.VMEM((window, rows), f32),
            dma((ring_sems,)), dma((ring_sems,)),
            dma((6,)), dma((6,)),
            dma((4,)), dma((4,)),
        ],
        compiler_params=pltpu.CompilerParams(
            collective_id=0, has_side_effects=True, vmem_limit_bytes=48 * 1024 * 1024
        ),
        cost_estimate=pl.CostEstimate(
            flops=2 * rows * width * (2 * window + 3 * model), bytes_accessed=8 * 1024 * 1024,
            transcendentals=rows * window * HEADS,
        ),
        name="semantic_part",
    )(queries, keys, values, inputs, gain, out_proj, key_proj, value_proj, counts)


def on_device(
    n, sem_queries, sem_keys, sem_values, sem_inputs, out_proj, norm_gain, key_proj, value_proj,
    slopes, coarse_queries, counts, band_bounds,
):
    near_keys, near_values, start = semantic_part(
        n, sem_queries, sem_keys, sem_values, sem_inputs, norm_gain[None, :], out_proj, key_proj,
        value_proj, jnp.broadcast_to(counts[:, None], (8, 128)),
    )
    return cross_attention(
        band_bounds, start, counts, slopes, coarse_queries, near_keys, near_values
    )


def solution(mesh):
    return jax.shard_map(
        functools.partial(on_device, mesh.shape["ctx"]),
        mesh=mesh,
        in_specs=(
            P(("groups", "ctx"), None),
            P(("groups", "ctx"), None),
            P(("groups", "ctx"), None),
            P(("groups", "ctx"), None),
            P("ctx", None),
            P(),
            P("ctx", None),
            P("ctx", None),
            P(),
            P(("groups", "ctx"), None),
            P(("groups", "ctx")),
            P(("groups", "ctx"), None),
        ),
        out_specs=P(("groups", "ctx"), None),
        check_vma=False,
    )
```
